32 devices in a mesh: group: 2 (over y), expert: 8 (over z, x), tensor: 2 (over core).
Axes of the slice: x: 2, y: 2, z: 4, core: 2. Of those that a mesh axis runs over, the one named last changes fastest.
Arguments:
- tokens: bfloat16 [256, 6144], P(('group', 'expert', 'tensor')), parts along dimension 0, may hold values from -6 to 6
- routes: int32 [256, 4], P(('group', 'expert', 'tensor')), parts along dimension 0, may hold values from 0 to 7, all different within a row; in each aligned block of 8 rows (0 to 7, 8 to 15, ...) at most 8 rows name the same one
- gate_fixed: int32 [256, 4], P(('group', 'expert', 'tensor')), parts along dimension 0, may hold values from 1 to 65535
- w_gate: bfloat16 [8, 6144, 5376], P('expert', None, 'tensor'), may hold values from -0.078125 to 0.078125
- w_up: bfloat16 [8, 6144, 5376], P('expert', None, 'tensor'), may hold values from -0.078125 to 0.078125
- w_down: bfloat16 [8, 5376, 6144], P('expert', 'tensor'), may hold values from -0.078125 to 0.078125
Outputs:
- mixed: bfloat16 [256, 6144], P(('group', 'expert', 'tensor')), parts along dimension 0
The draws below stay inside these ranges and needn't reach their ends.
There are 2 independent parts, one for each index of `group`. The reference program is written for one: setup_inputs(seed, part) draws one part's arguments, and reference() takes and returns one part's arrays. A program takes and returns all parts, laid end to end along the dimension named above; an argument that names none is the same for every part. Nothing has to cross between parts.
Inputs may be any that keep to these rules, and one draw needn't show every extreme that they name: `routes`: each row names 4 different experts. Among the 8 rows of one device no expert is named more than 8 times, and in some device an expert is named exactly 8 times.
All inputs are finite; a program needn't handle non-finite values.
Results may differ from the reference program's by a relative error of at most 0.0065.
Values may be sent and summed in bfloat16 or wider, within the bound.
A program may use at most 192 MiB of HBM per device.

```python
import math
import jax
import jax.numpy as jnp
import numpy as np
from jax import lax

D = 6144
FF = 5376
TOP = 4
TOK_DEV = 8
CAP = 8
EXPERTS = 8
TOKENS = 128
N_TENSOR = 2


def touch_ends(entries, stream_key, low, top_value):
    longest = entries.shape.index(max(entries.shape))
    spots = []
    for shift in (0, 1):
        where = [jax.random.randint(jax.random.fold_in(stream_key, axis), (), 0, length) for axis, length in enumerate(entries.shape)]
        where[longest] = (where[longest] + shift) % entries.shape[longest]
        spots.append(tuple(where))
    return entries.at[spots[0]].set(low).at[spots[1]].set(top_value)


def block_levels(stream_key, extent, shards, low, largest):
    gain = 1.0
    for dim, parts in shards:
        heights = jax.random.uniform(jax.random.fold_in(jax.random.fold_in(stream_key, 6), dim), (parts,), jnp.float32, low / len(shards), largest / len(shards))
        gain = gain * jnp.repeat(jnp.exp(heights), extent[dim] // parts).reshape((-1,) + (1,) * (len(extent) - 1 - dim))
    return gain


def shared_out(rng, own, number, rows, amount, top, most, slope):
    order = jax.random.permutation(rng, amount)
    crowded, usual = portions_of(amount, rows * top, most, slope, True), portions_of(amount, rows * top, most, slope, False)
    places = jnp.arange(amount)

    def named(tallies, offset_by):
        used = int((tallies > 0).sum())
        fixed = max(1, used // 4)
        passed = fixed + (places - fixed + offset_by * (used - fixed)) % max(1, amount - fixed)
        return jnp.zeros((amount,), jnp.int32).at[order[jnp.where(places < fixed, places, passed)]].set(jnp.asarray(tallies, jnp.int32))

    tallies = jnp.where(number % 4 == 0, named(crowded, number // 4), named(usual, number - number // 4 - 1))
    mixed = jax.random.permutation(jax.random.fold_in(own, 3), amount)
    giver, receiver = mixed[0:amount // 2 * 2:2], mixed[1:amount // 2 * 2:2]
    room = jnp.minimum(tallies[giver] - 1, most - tallies[receiver]) // 2
    room = jnp.where((giver == order[0]) | (receiver == order[0]) | (tallies[receiver] == 0), 0, jnp.maximum(room, 0))
    passed = jax.random.randint(jax.random.fold_in(own, 4), (amount // 2,), 0, 1 << 20) % (room + 1)
    tallies = tallies.at[giver].add(-passed).at[receiver].add(passed)
    items = jnp.searchsorted(jnp.cumsum(tallies), jnp.arange(rows * top), side="right").astype(jnp.int32)
    listing = items.reshape(top, rows).T
    listing = listing[jax.random.permutation(jax.random.fold_in(own, 1), rows)]
    offset_by = jax.random.randint(jax.random.fold_in(own, 2), (rows, 1), 0, top)
    return jnp.take_along_axis(listing, (jnp.arange(top)[None, :] + offset_by) % top, axis=1)


def portions_of(count, total, limit, lean, full):
    weights = [(1 << 20) // math.isqrt(rank ** lean) + 1 for rank in range(1, count + 1)]
    largest = limit if full else min(limit, max(-(-total // count), total * weights[0] // sum(weights)))
    least = 1 if total - largest >= count - 1 else 0
    given, spare = [largest] + [least] * (count - 1), total - largest - least * (count - 1)
    while spare > 0:
        candidates = [i for i in range(1, count) if given[i] < largest] or [i for i in range(1, count) if given[i] < limit]
        whole, budget = sum([weights[i] for i in candidates]), spare
        for i in candidates:
            extra = min(limit - given[i], max(1, budget * weights[i] // whole), spare)
            given[i] = given[i] + extra
            spare = spare - extra
    return np.array(given)


def scatter_about(rng, dims, spread, bound, split=(), kind=jnp.bfloat16):
    values = spread * jax.random.normal(rng, dims, jnp.float32)
    if split:
        values = values * block_levels(rng, dims, split, -0.22, 0.18)
    return jnp.clip(values, -bound, bound).astype(kind)


def setup_inputs(seed: int = 0, part: int = 0) -> dict:
    seeds = jax.random.split(jax.random.key(seed), 7)
    own_keys = jax.random.split(jax.random.fold_in(seeds[6], part), 7)
    tokens = scatter_about(own_keys[0], (TOKENS, D), 1.0, 6.0, ((0, 16),))
    routes_keys = jax.random.split(jax.random.fold_in(own_keys[1], 1), TOKENS // TOK_DEV)
    routes_turns = jax.random.permutation(jax.random.fold_in(own_keys[1], 3), TOKENS // TOK_DEV)
    routes = jax.vmap(lambda own, number: shared_out(jax.random.fold_in(own_keys[1], 2), own, number, TOK_DEV, EXPERTS, TOP, CAP, 2))(routes_keys, routes_turns).reshape((TOKENS, TOP))
    gate_fixed = touch_ends(jax.random.randint(own_keys[2], (TOKENS, TOP), 1, 65536), jax.random.fold_in(own_keys[2], 1), 1, 65535).astype(jnp.int32)
    w_gate = scatter_about(seeds[3], (EXPERTS, D, FF), D ** -0.5, 0.078125, ((0, 8), (2, 2)))
    w_up = scatter_about(seeds[4], (EXPERTS, D, FF), D ** -0.5, 0.078125, ((0, 8), (2, 2)))
    w_down = scatter_about(seeds[5], (EXPERTS, FF, D), FF ** -0.5, 0.078125, ((0, 8), (1, 2)))
    return {"tokens": tokens, "routes": routes, "gate_fixed": gate_fixed, "w_gate": w_gate, "w_up": w_up, "w_down": w_down}


def expert_output(tokens, gate_block, up_block, down_block):
    gate_val = jnp.dot(tokens, gate_block, preferred_element_type=jnp.float32)
    up_val = jnp.dot(tokens, up_block, preferred_element_type=jnp.float32)
    hidden = (jax.nn.silu(gate_val) * up_val).astype(jnp.bfloat16)
    shard_width = hidden.shape[1] // N_TENSOR
    hidden_parts = hidden.reshape(hidden.shape[0], N_TENSOR, shard_width).transpose(1, 0, 2)
    down_parts = down_block.reshape(N_TENSOR, shard_width, down_block.shape[1])

    def add_part(total, pair):
        partial_value = jnp.dot(pair[0], pair[1], preferred_element_type=jnp.float32).astype(jnp.bfloat16)
        partial_value = lax.optimization_barrier(partial_value)
        return total + partial_value.astype(jnp.float32), None

    start_sum = jnp.zeros((hidden.shape[0], down_block.shape[1]), jnp.float32)
    total, unused = lax.scan(add_part, start_sum, (hidden_parts, down_parts))
    return total.astype(jnp.bfloat16)


def reference(tokens, routes, gate_fixed, w_gate, w_up, w_down):
    fixed_val = gate_fixed.astype(jnp.float32)
    mix = fixed_val / jnp.sum(fixed_val, axis=1, keepdims=True)

    def per_expert(total, packed):
        index, gate_block, up_block, down_block = packed
        out_rows = expert_output(tokens, gate_block, up_block, down_block)
        coeff = jnp.sum(jnp.where(routes == index, mix, 0.0), axis=1)
        return total + coeff[:, None] * out_rows.astype(jnp.float32), None

    start_sum = jnp.zeros((TOKENS, D), jnp.float32)
    indices = jnp.arange(EXPERTS, dtype=jnp.int32)
    total, unused = lax.scan(per_expert, start_sum, (indices, w_gate, w_up, w_down))
    return total.astype(jnp.bfloat16)
```

```python
import functools

import jax
import jax.numpy as jnp
from jax import lax
from jax.experimental import pallas as pl
from jax.experimental.pallas import tpu as pltpu
from jax.sharding import PartitionSpec as P

CAP = 8
LANES = 128
K_SLOTS = 3
D_SLOTS = 6
MESH = pl.DeviceIdType.MESH


def divisor(n, most, unit):
    best = unit
    for d in range(unit, most + 1, unit):
        if n % d == 0:
            best = d
    return best


def pieces(n, width):
    return [(c, min(width, n - c)) for c in range(0, n, width)]


def fused_kernel(
    Z, X, T, KB, NB,
    tok_ref, routes_ref, gate_ref, wg_hbm, wu_hbm, wd_hbm, out_ref,
    xraw, xb, coef, wg, wu, wd, acc_g, acc_u, hid,
    part, got_a, send_b, own_b, got_b, send_c, got_c,
    wg_sem, wu_sem, wd_sem, xs_sem, xr_sem,
    as_sem, ar_sem, bs_sem, br_sem, cs_sem, cr_sem,
):
    E = Z * X
    R, D = tok_ref.shape
    F = wg_hbm.shape[2]
    ROWS = E * T * R
    KN = D // KB
    ND = D // NB
    e = lax.axis_index("expert")
    t = lax.axis_index("tensor")
    x = lax.rem(e, X)
    z = e // X
    xo = 1 - x
    to = 1 - t

    def gate_copies(k, slot):
        rows = pl.ds(pl.multiple_of(k * KB, KB), KB)
        return (
            pltpu.make_async_copy(wg_hbm.at[0, rows, :], wg.at[slot], wg_sem.at[slot]),
            pltpu.make_async_copy(wu_hbm.at[0, rows, :], wu.at[slot], wu_sem.at[slot]),
        )

    def down_copy(i, slot):
        cols = pl.ds(pl.multiple_of(i * NB, NB), NB)
        return pltpu.make_async_copy(wd_hbm.at[0, :, cols], wd.at[slot], wd_sem.at[slot])

    for k in range(K_SLOTS):
        for c in gate_copies(k, k):
            c.start()
    for i in range(D_SLOTS):
        down_copy(i, i).start()

    def block(tt, xx, zz):
        return tt * E + xx * Z + zz

    mine = block(t, x, z)
    zs = [lax.rem(z + d, Z) for d in range(Z)]
    at_z = [{"expert": zz * X + x, "tensor": t} for zz in zs]
    at_x = {"expert": z * X + xo, "tensor": t}
    at_t = {"expert": e, "tensor": to}
    peers = at_z[1:] + [at_x, at_t]

    barrier = pltpu.get_barrier_semaphore()
    for p in peers:
        pl.semaphore_signal(barrier, inc=1, device_id=p, device_id_type=MESH)

    fixed = gate_ref[...].astype(jnp.float32)
    mix = fixed / jnp.sum(fixed, axis=1, keepdims=True)
    routes = routes_ref[...]
    lane = lax.broadcasted_iota(jnp.int32, (R, LANES), 1)
    expert_of = lax.rem(lane, E)
    c = jnp.zeros((R, LANES), jnp.float32)
    for k in range(routes.shape[1]):
        c = c + jnp.where(expert_of == routes[:, k:k + 1], mix[:, k:k + 1], 0.0)
    hi = c.astype(jnp.bfloat16).astype(jnp.float32)
    mid = (c - hi).astype(jnp.bfloat16).astype(jnp.float32)
    low = c - hi - mid
    term = lane // E
    c = jnp.where(term == 0, hi, jnp.where(term == 1, mid, jnp.where(term == 2, low, 0.0)))
    xraw[mine, :, :D] = tok_ref[...]
    xraw[mine, :, D:] = c.astype(jnp.bfloat16)

    pl.semaphore_wait(barrier, len(peers))

    sent = []

    def send(b, where):
        n = len(sent)
        cp = pltpu.make_async_remote_copy(
            src_ref=xraw.at[b], dst_ref=xraw.at[b], send_sem=xs_sem.at[n], recv_sem=xr_sem.at[b],
            device_id=where, device_id_type=MESH)
        cp.start()
        sent.append(cp)

    def arrived(b):
        pltpu.make_async_remote_copy(
            src_ref=xraw.at[b], dst_ref=xraw.at[b], send_sem=xs_sem.at[0], recv_sem=xr_sem.at[b],
            device_id=at_t, device_id_type=MESH).wait_recv()

    send(mine, at_x)
    for d in range(1, Z):
        send(mine, at_z[d])
    send(mine, at_t)
    for d in range(1, Z):
        b = block(t, x, zs[d])
        arrived(b)
        send(b, at_x)
        send(b, at_t)
    for d in range(Z):
        b = block(t, xo, zs[d])
        arrived(b)
        send(b, at_t)
    for d in range(Z):
        arrived(block(to, x, zs[d]))
    for d in range(Z):
        arrived(block(to, xo, zs[d]))

    @pl.loop(0, E * T // 2)
    def _(p):
        rows = pl.ds(pl.multiple_of(p * 2 * R, 2 * R), 2 * R)
        for c0, w in pieces(D, 1024):
            two = xraw[pl.ds(p * 2, 2), :, c0:c0 + w].astype(jnp.float32)
            xb[rows, c0:c0 + w] = two.reshape(2 * R, w).astype(jnp.bfloat16)
        two = xraw[pl.ds(p * 2, 2), :, D:].astype(jnp.float32).reshape(2 * R, LANES)
        at = lax.broadcasted_iota(jnp.int32, (2 * R, LANES), 1)
        own = jnp.where((lax.rem(at, E) == e) & (at < 3 * E), two, 0.0)
        coef[rows, :] = jnp.broadcast_to(jnp.sum(own, axis=1, keepdims=True), (2 * R, LANES))

    for c0, w in pieces(F, 512):
        acc_g[:, c0:c0 + w] = jnp.zeros((ROWS, w), jnp.float32)
        acc_u[:, c0:c0 + w] = jnp.zeros((ROWS, w), jnp.float32)

    @pl.loop(0, KN)
    def _(k):
        slot = lax.rem(k, K_SLOTS)
        xk = xb[:, pl.ds(pl.multiple_of(k * KB, KB), KB)]
        for cp, w_ref, acc in zip(gate_copies(k, slot), (wg, wu), (acc_g, acc_u)):
            cp.wait()
            for c0, w in pieces(F, 512):
                acc[:, c0:c0 + w] += jnp.dot(
                    xk, w_ref[slot, :, c0:c0 + w], preferred_element_type=jnp.float32)

        @pl.when(k + K_SLOTS < KN)
        def _():
            for cp in gate_copies(k + K_SLOTS, slot):
                cp.start()

    for c0, w in pieces(F, 512):
        g = acc_g[:, c0:c0 + w]
        hid[:, c0:c0 + w] = (g / (1.0 + jnp.exp(-g)) * acc_u[:, c0:c0 + w]).astype(jnp.bfloat16)

    def copy_a(i):
        return pltpu.make_async_remote_copy(
            src_ref=part.at[i, to], dst_ref=got_a.at[i], send_sem=as_sem.at[i], recv_sem=ar_sem.at[i],
            device_id=at_t, device_id_type=MESH)

    def copy_b(i):
        return pltpu.make_async_remote_copy(
            src_ref=send_b.at[i], dst_ref=got_b.at[i], send_sem=bs_sem.at[i], recv_sem=br_sem.at[i],
            device_id=at_x, device_id_type=MESH)

    def copy_c(i, d):
        return pltpu.make_async_remote_copy(
            src_ref=send_c.at[i, zs[d]], dst_ref=got_c.at[i, d - 1],
            send_sem=cs_sem.at[i, d - 1], recv_sem=cr_sem.at[i, d - 1],
            device_id=at_z[d], device_id_type=MESH)

    LAG_A, LAG_B, LAG_C = 1, 3, 5

    @pl.loop(0, ND + LAG_C)
    def _(i):
        @pl.when(i < ND)
        def _():
            slot = lax.rem(i, D_SLOTS)
            down_copy(i, slot).wait()
            y = jnp.dot(hid[...], wd[slot], preferred_element_type=jnp.float32) * coef[:, 0:1]
            part[i] = y.reshape(T, E, R, NB).astype(jnp.bfloat16)
            copy_a(i).start()

            @pl.when(i + D_SLOTS < ND)
            def _():
                down_copy(i + D_SLOTS, slot).start()

        @pl.when((i >= LAG_A) & (i < ND + LAG_A))
        def _():
            j = i - LAG_A
            copy_a(j).wait_recv()
            theirs = pl.ds(xo * Z, Z)
            ours = pl.ds(x * Z, Z)
            send_b[j] = (part[j, t, theirs].astype(jnp.float32)
                         + got_a[j, theirs].astype(jnp.float32)).astype(jnp.bfloat16)
            copy_b(j).start()
            own_b[j] = part[j, t, ours].astype(jnp.float32) + got_a[j, ours].astype(jnp.float32)

        @pl.when((i >= LAG_B) & (i < ND + LAG_B))
        def _():
            j = i - LAG_B
            copy_b(j).wait_recv()
            send_c[j] = (own_b[j] + got_b[j].astype(jnp.float32)).astype(jnp.bfloat16)
            for d in range(1, Z):
                copy_c(j, d).start()

        @pl.when(i >= LAG_C)
        def _():
            j = i - LAG_C
            total = send_c[j, z].astype(jnp.float32)
            for d in range(1, Z):
                copy_c(j, d).wait_recv()
                total = total + got_c[j, d - 1].astype(jnp.float32)
            out_ref[:, pl.ds(pl.multiple_of(j * NB, NB), NB)] = total.astype(jnp.bfloat16)

    for cp in sent:
        cp.wait_send()

    @pl.loop(0, ND)
    def _(i):
        copy_a(i).wait_send()
        copy_b(i).wait_send()
        for d in range(1, Z):
            copy_c(i, d).wait_send()


def fused_shards(tokens, routes, gate_fixed, w_gate, w_up, w_down):
    E, T = lax.axis_size("expert"), lax.axis_size("tensor")
    X = 2
    Z = E // X
    R, D = tokens.shape
    F = w_gate.shape[2]
    KB = divisor(D, 768, 256)
    NB = divisor(D, 512, 256)
    ND = D // NB
    rows = E * T * R
    bf, f32 = jnp.bfloat16, jnp.float32
    vm = pltpu.VMEM
    dma = pltpu.SemaphoreType.DMA
    vmem, any_ = pl.BlockSpec(memory_space=vm), pl.BlockSpec(memory_space=pl.ANY)
    return pl.pallas_call(
        functools.partial(fused_kernel, Z, X, T, KB, NB),
        out_shape=jax.ShapeDtypeStruct((R, D), bf),
        in_specs=[vmem, vmem, vmem, any_, any_, any_],
        out_specs=vmem,
        scratch_shapes=[
            vm((E * T, R, D + LANES), bf),
            vm((rows, D), bf),
            vm((rows, LANES), f32),
            vm((K_SLOTS, KB, F), bf),
            vm((K_SLOTS, KB, F), bf),
            vm((D_SLOTS, F, NB), bf),
            vm((rows, F), f32),
            vm((rows, F), f32),
            vm((rows, F), bf),
            vm((ND, T, E, R, NB), bf),
            vm((ND, E, R, NB), bf),
            vm((ND, Z, R, NB), bf),
            vm((ND, Z, R, NB), f32),
            vm((ND, Z, R, NB), bf),
            vm((ND, Z, R, NB), bf),
            vm((ND, Z - 1, R, NB), bf),
            dma((K_SLOTS,)), dma((K_SLOTS,)), dma((D_SLOTS,)),
            dma((E * T - 1,)), dma((E * T,)),
            dma((ND,)), dma((ND,)), dma((ND,)), dma((ND,)), dma((ND, Z - 1)), dma((ND, Z - 1)),
        ],
        compiler_params=pltpu.CompilerParams(
            collective_id=0, has_side_effects=True, vmem_limit_bytes=60 * 1024 * 1024),
        cost_estimate=pl.CostEstimate(
            flops=6 * rows * D * F, bytes_accessed=6 * D * F, transcendentals=rows * F),
    )(tokens, routes, gate_fixed, w_gate, w_up, w_down)


def slot_table(route_block, n_experts):
    flat_ids = route_block.reshape(-1)
    onehot = (flat_ids[:, None] == jnp.arange(n_experts, dtype=jnp.int32)[None, :]).astype(
        jnp.int32
    )
    earlier = jnp.cumsum(onehot, axis=0) - onehot
    slot_pos = jnp.sum(earlier * onehot, axis=1)
    target = flat_ids * CAP + slot_pos
    owner_row = jnp.arange(flat_ids.shape[0], dtype=jnp.int32) // route_block.shape[1]
    source = jnp.full((n_experts * CAP,), -1, jnp.int32).at[target].set(owner_row)
    return (source, target)


def pick_rows(table, source):
    picked = jnp.take(table, jnp.maximum(source, 0), axis=0)
    return jnp.where((source >= 0)[..., None], picked, jnp.zeros_like(picked))


def shards(tokens, routes, gate_fixed, w_gate, w_up, w_down):
    n_experts = lax.axis_size("expert")
    model_width = tokens.shape[1]
    gate_mat = w_gate[0]
    up_mat = w_up[0]
    down_mat = w_down[0]
    source, target = slot_table(routes, n_experts)
    outgoing = pick_rows(tokens, source.reshape(n_experts, CAP))
    arrived = lax.all_to_all(outgoing, "expert", split_axis=0, concat_axis=0, tiled=True)
    row_piece = lax.all_gather(arrived.reshape(-1, model_width), "tensor", axis=0, tiled=True)
    gate_val = jnp.dot(row_piece, gate_mat, preferred_element_type=jnp.float32)
    up_val = jnp.dot(row_piece, up_mat, preferred_element_type=jnp.float32)
    hidden = (jax.nn.silu(gate_val) * up_val).astype(jnp.bfloat16)
    shared_sum = lax.psum_scatter(
        jnp.dot(hidden, down_mat, preferred_element_type=jnp.float32).astype(jnp.bfloat16),
        "tensor",
        scatter_dimension=0,
        tiled=True,
    )
    expert_rows = shared_sum.reshape(n_experts, CAP, model_width)
    returned = lax.all_to_all(expert_rows, "expert", split_axis=0, concat_axis=0, tiled=True)
    chosen = jnp.take(returned.reshape(-1, model_width), target, axis=0)
    chosen = chosen.reshape(tokens.shape[0], routes.shape[1], model_width)
    fixed_val = gate_fixed.astype(jnp.float32)
    mix_weights = fixed_val / jnp.sum(fixed_val, axis=1, keepdims=True)
    mixed = jnp.sum(chosen.astype(jnp.float32) * mix_weights[:, :, None], axis=1)
    return mixed.astype(jnp.bfloat16)


def solution(mesh):
    placed = (
        P(("group", "expert", "tensor"), None),
        P(("group", "expert", "tensor"), None),
        P(("group", "expert", "tensor"), None),
        P("expert", None, "tensor"),
        P("expert", None, "tensor"),
        P("expert", "tensor", None),
    )
    fits = (mesh.shape["tensor"] == 2 and mesh.shape["expert"] % 4 == 0)
    return jax.shard_map(
        fused_shards if fits else shards,
        mesh=mesh,
        in_specs=placed,
        out_specs=P(("group", "expert", "tensor"), None),
        check_vma=False,
    )
```

```python
import functools

import jax
import jax.numpy as jnp
from jax import lax
from jax.experimental import pallas as pl
from jax.experimental.pallas import tpu as pltpu
from jax.sharding import PartitionSpec as P

CAP = 8
LANES = 128
K_SLOTS = 4
D_SLOTS = 4
STEPS = 2
MESH = pl.DeviceIdType.MESH


def divisor(n, most, unit):
    best = unit
    for d in range(unit, most + 1, unit):
        if n % d == 0:
            best = d
    return best


def pieces(n, width):
    return [(c, min(width, n - c)) for c in range(0, n, width)]


def fused_kernel(
    Z, X, T, KB, NB,
    tok_ref, routes_ref, gate_ref, wg_hbm, wu_hbm, wd_hbm, out_ref,
    xraw, xb, coef, wg, wu, wd, acc_g, acc_u, hid,
    part, got_a, send_b, own_b, got_b, send_c, got_c,
    wg_sem, wu_sem, wd_sem, xs_sem, xr_sem,
    as_sem, ar_sem, bs_sem, br_sem, cs_sem, cr_sem,
):
    E = Z * X
    R, D = tok_ref.shape
    F = wg_hbm.shape[2]
    ROWS = E * T * R
    KN = D // KB
    ND = D // NB
    CW = STEPS * KB
    CN = D // CW
    e = lax.axis_index("expert")
    t = lax.axis_index("tensor")
    x = lax.rem(e, X)
    z = e // X
    xo = 1 - x
    to = 1 - t

    def gate_copies(k, slot):
        rows = pl.ds(pl.multiple_of(k * KB, KB), KB)
        return (
            pltpu.make_async_copy(wg_hbm.at[0, rows, :], wg.at[slot], wg_sem.at[slot]),
            pltpu.make_async_copy(wu_hbm.at[0, rows, :], wu.at[slot], wu_sem.at[slot]),
        )

    def down_copy(i, slot):
        cols = pl.ds(pl.multiple_of(i * NB, NB), NB)
        return pltpu.make_async_copy(wd_hbm.at[0, :, cols], wd.at[slot], wd_sem.at[slot])

    for k in range(K_SLOTS):
        for c in gate_copies(k, k):
            c.start()

    def block(tt, xx, zz):
        return tt * E + xx * Z + zz

    mine = block(t, x, z)
    zs = [lax.rem(z + d, Z) for d in range(Z)]
    at_z = [{"expert": zz * X + x, "tensor": t} for zz in zs]
    at_x = {"expert": z * X + xo, "tensor": t}
    at_t = {"expert": e, "tensor": to}
    peers = at_z[1:] + [at_x, at_t]

    barrier = pltpu.get_barrier_semaphore()
    for p in peers:
        pl.semaphore_signal(barrier, inc=1, device_id=p, device_id_type=MESH)

    fixed = gate_ref[...].astype(jnp.float32)
    mix = fixed / jnp.sum(fixed, axis=1, keepdims=True)
    routes = routes_ref[...]
    lane = lax.broadcasted_iota(jnp.int32, (R, LANES), 1)
    expert_of = lax.rem(lane, E)
    c = jnp.zeros((R, LANES), jnp.float32)
    for k in range(routes.shape[1]):
        c = c + jnp.where(expert_of == routes[:, k:k + 1], mix[:, k:k + 1], 0.0)
    hi = c.astype(jnp.bfloat16).astype(jnp.float32)
    mid = (c - hi).astype(jnp.bfloat16).astype(jnp.float32)
    low = c - hi - mid
    term = lane // E
    c = jnp.where(term == 0, hi, jnp.where(term == 1, mid, jnp.where(term == 2, low, 0.0)))
    for n in range(CN):
        xraw[n, mine, :, :CW] = tok_ref[:, n * CW:(n + 1) * CW]
        xraw[n, mine, :, CW:] = c.astype(jnp.bfloat16)

    pl.semaphore_wait(barrier, len(peers))

    from_own = [(mine, at_z[1]), (mine, at_x)] + [(mine, at_z[d]) for d in range(2, Z)] + [(mine, at_t)]
    from_z = [(block(t, x, zs[d]), w) for d in range(1, Z) for w in (at_x, at_t)]
    from_x = [(block(t, xo, zs[d]), at_t) for d in range(Z)]
    from_t = [block(to, xx, zs[d]) for xx in (x, xo) for d in range(Z)]
    routes_out = from_own + from_z + from_x

    def token_copy(n, k):
        b, where = routes_out[k]
        return pltpu.make_async_remote_copy(
            src_ref=xraw.at[n, b], dst_ref=xraw.at[n, b], send_sem=xs_sem.at[n, k], recv_sem=xr_sem.at[n, b],
            device_id=where, device_id_type=MESH)

    def arrived(n, b):
        pltpu.make_async_remote_copy(
            src_ref=xraw.at[n, b], dst_ref=xraw.at[n, b], send_sem=xs_sem.at[n, 0], recv_sem=xr_sem.at[n, b],
            device_id=at_t, device_id_type=MESH).wait_recv()

    def pass_z(n):
        k = len(from_own)
        for d in range(1, Z):
            arrived(n, block(t, x, zs[d]))
            token_copy(n, k).start()
            token_copy(n, k + 1).start()
            k += 2

    def pass_x(n):
        k = len(from_own) + len(from_z)
        for d in range(Z):
            arrived(n, block(t, xo, zs[d]))
            token_copy(n, k).start()
            k += 1

    for n in range(CN):
        for k in range(len(from_own)):
            token_copy(n, k).start()
    for c0, w in pieces(F, 512):
        acc_g[:, c0:c0 + w] = jnp.zeros((ROWS, w), jnp.float32)
        acc_u[:, c0:c0 + w] = jnp.zeros((ROWS, w), jnp.float32)
    pass_z(0)
    if CN > 1:
        pass_z(1)
    pass_x(0)

    @pl.loop(0, CN)
    def _(n):
        for b in from_t:
            arrived(n, b)

        @pl.loop(0, E * T // 2)
        def _(p):
            rows = pl.ds(pl.multiple_of(p * 2 * R, 2 * R), 2 * R)
            for j in range(STEPS):
                two = xraw[n, pl.ds(p * 2, 2), :, j * KB:(j + 1) * KB].astype(jnp.float32)
                xb[j, rows, :] = two.reshape(2 * R, KB).astype(jnp.bfloat16)

        for j in range(STEPS):
            k = n * STEPS + j
            slot = lax.rem(k, K_SLOTS)
            for cp, w_ref, acc in zip(gate_copies(k, slot), (wg, wu), (acc_g, acc_u)):
                cp.wait()
                for c0, w in pieces(F, 512):
                    acc[:, c0:c0 + w] += jnp.dot(
                        xb[j], w_ref[slot, :, c0:c0 + w], preferred_element_type=jnp.float32)

            @pl.when(k + K_SLOTS < KN)
            def _():
                for cp in gate_copies(k + K_SLOTS, slot):
                    cp.start()

            @pl.when(k + K_SLOTS == KN - 1)
            def _():
                for i in range(D_SLOTS):
                    down_copy(i, i).start()

            if j == 0:
                @pl.when(n + 1 < CN)
                def _():
                    pass_x(n + 1)

                @pl.when(n + 2 < CN)
                def _():
                    pass_z(n + 2)

    @pl.loop(0, E * T // 2)
    def _(p):
        rows = pl.ds(pl.multiple_of(p * 2 * R, 2 * R), 2 * R)
        two = xraw[0, pl.ds(p * 2, 2), :, CW:].astype(jnp.float32).reshape(2 * R, LANES)
        at = lax.broadcasted_iota(jnp.int32, (2 * R, LANES), 1)
        own = jnp.where((lax.rem(at, E) == e) & (at < 3 * E), two, 0.0)
        coef[rows, :] = jnp.broadcast_to(jnp.sum(own, axis=1, keepdims=True), (2 * R, LANES))

    for c0, w in pieces(F, 512):
        g = acc_g[:, c0:c0 + w]
        hid[:, c0:c0 + w] = (g / (1.0 + jnp.exp(-g)) * acc_u[:, c0:c0 + w]).astype(jnp.bfloat16)

    def copy_a(i):
        return pltpu.make_async_remote_copy(
            src_ref=part.at[i, to], dst_ref=got_a.at[i], send_sem=as_sem.at[i], recv_sem=ar_sem.at[i],
            device_id=at_t, device_id_type=MESH)

    def copy_b(i):
        return pltpu.make_async_remote_copy(
            src_ref=send_b.at[i], dst_ref=got_b.at[i], send_sem=bs_sem.at[i], recv_sem=br_sem.at[i],
            device_id=at_x, device_id_type=MESH)

    def copy_c(i, d):
        return pltpu.make_async_remote_copy(
            src_ref=send_c.at[i, zs[d]], dst_ref=got_c.at[i, d - 1],
            send_sem=cs_sem.at[i, d - 1], recv_sem=cr_sem.at[i, d - 1],
            device_id=at_z[d], device_id_type=MESH)

    LAG_A, LAG_B, LAG_C = 2, 5, 8

    @pl.loop(0, ND + LAG_C)
    def _(i):
        @pl.when(i < ND)
        def _():
            slot = lax.rem(i, D_SLOTS)
            down_copy(i, slot).wait()
            y = jnp.dot(hid[...], wd[slot], preferred_element_type=jnp.float32) * coef[:, 0:1]
            part[i] = y.reshape(T, E, R, NB).astype(jnp.bfloat16)
            copy_a(i).start()

            @pl.when(i + D_SLOTS < ND)
            def _():
                down_copy(i + D_SLOTS, slot).start()

        @pl.when((i >= LAG_A) & (i < ND + LAG_A))
        def _():
            j = i - LAG_A
            copy_a(j).wait_recv()
            theirs = pl.ds(xo * Z, Z)
            ours = pl.ds(x * Z, Z)
            send_b[j] = (part[j, t, theirs].astype(jnp.float32)
                         + got_a[j, theirs].astype(jnp.float32)).astype(jnp.bfloat16)
            copy_b(j).start()
            own_b[j] = part[j, t, ours].astype(jnp.float32) + got_a[j, ours].astype(jnp.float32)

        @pl.when((i >= LAG_B) & (i < ND + LAG_B))
        def _():
            j = i - LAG_B
            copy_b(j).wait_recv()
            send_c[j] = (own_b[j] + got_b[j].astype(jnp.float32)).astype(jnp.bfloat16)
            for d in range(1, Z):
                copy_c(j, d).start()

        @pl.when(i >= LAG_C)
        def _():
            j = i - LAG_C
            total = send_c[j, z].astype(jnp.float32)
            for d in range(1, Z):
                copy_c(j, d).wait_recv()
                total = total + got_c[j, d - 1].astype(jnp.float32)
            out_ref[:, pl.ds(pl.multiple_of(j * NB, NB), NB)] = total.astype(jnp.bfloat16)

    @pl.loop(0, CN)
    def _(n):
        for k in range(len(routes_out)):
            token_copy(n, k).wait_send()

    @pl.loop(0, ND)
    def _(i):
        copy_a(i).wait_send()
        copy_b(i).wait_send()
        for d in range(1, Z):
            copy_c(i, d).wait_send()


def fused_shards(tokens, routes, gate_fixed, w_gate, w_up, w_down):
    E, T = lax.axis_size("expert"), lax.axis_size("tensor")
    X = 2
    Z = E // X
    R, D = tokens.shape
    F = w_gate.shape[2]
    KB = divisor(D, 768, 256)
    NB = divisor(D, 512, 256)
    ND = D // NB
    CW = STEPS * KB
    CN = D // CW
    rows = E * T * R
    bf, f32 = jnp.bfloat16, jnp.float32
    vm = pltpu.VMEM
    dma = pltpu.SemaphoreType.DMA
    vmem, any_ = pl.BlockSpec(memory_space=vm), pl.BlockSpec(memory_space=pl.ANY)
    return pl.pallas_call(
        functools.partial(fused_kernel, Z, X, T, KB, NB),
        out_shape=jax.ShapeDtypeStruct((R, D), bf),
        in_specs=[vmem, vmem, vmem, any_, any_, any_],
        out_specs=vmem,
        scratch_shapes=[
            vm((CN, E * T, R, CW + LANES), bf),
            vm((STEPS, rows, KB), bf),
            vm((rows, LANES), f32),
            vm((K_SLOTS, KB, F), bf),
            vm((K_SLOTS, KB, F), bf),
            vm((D_SLOTS, F, NB), bf),
            vm((rows, F), f32),
            vm((rows, F), f32),
            vm((rows, F), bf),
            vm((ND, T, E, R, NB), bf),
            vm((ND, E, R, NB), bf),
            vm((ND, Z, R, NB), bf),
            vm((ND, Z, R, NB), f32),
            vm((ND, Z, R, NB), bf),
            vm((ND, Z, R, NB), bf),
            vm((ND, Z - 1, R, NB), bf),
            dma((K_SLOTS,)), dma((K_SLOTS,)), dma((D_SLOTS,)),
            dma((CN, E * T - 1)), dma((CN, E * T)),
            dma((ND,)), dma((ND,)), dma((ND,)), dma((ND,)), dma((ND, Z - 1)), dma((ND, Z - 1)),
        ],
        compiler_params=pltpu.CompilerParams(
            collective_id=0, has_side_effects=True, vmem_limit_bytes=61 * 1024 * 1024),
        cost_estimate=pl.CostEstimate(
            flops=6 * rows * D * F, bytes_accessed=6 * D * F, transcendentals=rows * F),
    )(tokens, routes, gate_fixed, w_gate, w_up, w_down)


def slot_table(route_block, n_experts):
    flat_ids = route_block.reshape(-1)
    onehot = (flat_ids[:, None] == jnp.arange(n_experts, dtype=jnp.int32)[None, :]).astype(
        jnp.int32
    )
    earlier = jnp.cumsum(onehot, axis=0) - onehot
    slot_pos = jnp.sum(earlier * onehot, axis=1)
    target = flat_ids * CAP + slot_pos
    owner_row = jnp.arange(flat_ids.shape[0], dtype=jnp.int32) // route_block.shape[1]
    source = jnp.full((n_experts * CAP,), -1, jnp.int32).at[target].set(owner_row)
    return (source, target)


def pick_rows(table, source):
    picked = jnp.take(table, jnp.maximum(source, 0), axis=0)
    return jnp.where((source >= 0)[..., None], picked, jnp.zeros_like(picked))


def shards(tokens, routes, gate_fixed, w_gate, w_up, w_down):
    n_experts = lax.axis_size("expert")
    model_width = tokens.shape[1]
    gate_mat = w_gate[0]
    up_mat = w_up[0]
    down_mat = w_down[0]
    source, target = slot_table(routes, n_experts)
    outgoing = pick_rows(tokens, source.reshape(n_experts, CAP))
    arrived = lax.all_to_all(outgoing, "expert", split_axis=0, concat_axis=0, tiled=True)
    row_piece = lax.all_gather(arrived.reshape(-1, model_width), "tensor", axis=0, tiled=True)
    gate_val = jnp.dot(row_piece, gate_mat, preferred_element_type=jnp.float32)
    up_val = jnp.dot(row_piece, up_mat, preferred_element_type=jnp.float32)
    hidden = (jax.nn.silu(gate_val) * up_val).astype(jnp.bfloat16)
    shared_sum = lax.psum_scatter(
        jnp.dot(hidden, down_mat, preferred_element_type=jnp.float32).astype(jnp.bfloat16),
        "tensor",
        scatter_dimension=0,
        tiled=True,
    )
    expert_rows = shared_sum.reshape(n_experts, CAP, model_width)
    returned = lax.all_to_all(expert_rows, "expert", split_axis=0, concat_axis=0, tiled=True)
    chosen = jnp.take(returned.reshape(-1, model_width), target, axis=0)
    chosen = chosen.reshape(tokens.shape[0], routes.shape[1], model_width)
    fixed_val = gate_fixed.astype(jnp.float32)
    mix_weights = fixed_val / jnp.sum(fixed_val, axis=1, keepdims=True)
    mixed = jnp.sum(chosen.astype(jnp.float32) * mix_weights[:, :, None], axis=1)
    return mixed.astype(jnp.bfloat16)


def solution(mesh):
    placed = (
        P(("group", "expert", "tensor"), None),
        P(("group", "expert", "tensor"), None),
        P(("group", "expert", "tensor"), None),
        P("expert", None, "tensor"),
        P("expert", None, "tensor"),
        P("expert", "tensor", None),
    )
    fits = (mesh.shape["tensor"] == 2 and mesh.shape["expert"] % 4 == 0)
    return jax.shard_map(
        fused_shards if fits else shards,
        mesh=mesh,
        in_specs=placed,
        out_specs=P(("group", "expert", "tensor"), None),
        check_vma=False,
    )
```

```python
import functools

import jax
import jax.numpy as jnp
from jax import lax
from jax.experimental import pallas as pl
from jax.experimental.pallas import tpu as pltpu
from jax.sharding import PartitionSpec as P

CAP = 8
LANES = 128
K_SLOTS = 4
D_SLOTS = 3
STEPS = 2
MESH = pl.DeviceIdType.MESH


def divisor(n, most, unit):
    best = unit
    for d in range(unit, most + 1, unit):
        if n % d == 0:
            best = d
    return best


def pieces(n, width):
    return [(c, min(width, n - c)) for c in range(0, n, width)]


def fused_kernel(
    Z, X, T, KB, NB,
    tok_ref, routes_ref, gate_ref, wg_hbm, wu_hbm, wd_hbm, out_ref,
    xraw, xb, coef, wg, wu, wd, acc_g, acc_u, hid,
    part, got_a, send_b, own_b, got_b, send_c, got_c,
    wg_sem, wu_sem, wd_sem, xs_sem, xr_sem,
    as_sem, ar_sem, bs_sem, br_sem, cs_sem, cr_sem,
):
    E = Z * X
    R, D = tok_ref.shape
    F = wg_hbm.shape[2]
    ROWS = E * T * R
    KN = D // KB
    ND = D // NB
    CW = STEPS * KB
    CN = D // CW
    e = lax.axis_index("expert")
    t = lax.axis_index("tensor")
    x = lax.rem(e, X)
    z = e // X
    xo = 1 - x
    to = 1 - t

    def gate_copies(k, slot):
        rows = pl.ds(pl.multiple_of(k * KB, KB), KB)
        return (
            pltpu.make_async_copy(wg_hbm.at[0, rows, :], wg.at[slot], wg_sem.at[slot]),
            pltpu.make_async_copy(wu_hbm.at[0, rows, :], wu.at[slot], wu_sem.at[slot]),
        )

    def down_copy(i, slot):
        cols = pl.ds(pl.multiple_of(i * NB, NB), NB)
        return pltpu.make_async_copy(wd_hbm.at[0, :, cols], wd.at[slot], wd_sem.at[slot])

    for k in range(K_SLOTS):
        for c in gate_copies(k, k):
            c.start()

    def block(tt, xx, zz):
        return tt * E + xx * Z + zz

    mine = block(t, x, z)
    zs = [lax.rem(z + d, Z) for d in range(Z)]
    at_z = [{"expert": zz * X + x, "tensor": t} for zz in zs]
    at_x = {"expert": z * X + xo, "tensor": t}
    at_t = {"expert": e, "tensor": to}
    peers = at_z[1:] + [at_x, at_t]

    barrier = pltpu.get_barrier_semaphore()
    for p in peers:
        pl.semaphore_signal(barrier, inc=1, device_id=p, device_id_type=MESH)

    fixed = gate_ref[...].astype(jnp.float32)
    mix = fixed / jnp.sum(fixed, axis=1, keepdims=True)
    routes = routes_ref[...]
    lane = lax.broadcasted_iota(jnp.int32, (R, LANES), 1)
    expert_of = lax.rem(lane, E)
    c = jnp.zeros((R, LANES), jnp.float32)
    for k in range(routes.shape[1]):
        c = c + jnp.where(expert_of == routes[:, k:k + 1], mix[:, k:k + 1], 0.0)
    hi = c.astype(jnp.bfloat16).astype(jnp.float32)
    mid = (c - hi).astype(jnp.bfloat16).astype(jnp.float32)
    low = c - hi - mid
    term = lane // E
    c = jnp.where(term == 0, hi, jnp.where(term == 1, mid, jnp.where(term == 2, low, 0.0)))
    for n in range(CN):
        xraw[n, mine, :, :CW] = tok_ref[:, n * CW:(n + 1) * CW]
        xraw[n, mine, :, CW:] = c.astype(jnp.bfloat16)

    pl.semaphore_wait(barrier, len(peers))

    from_own = [(mine, at_z[1]), (mine, at_x)] + [(mine, at_z[d]) for d in range(2, Z)] + [(mine, at_t)]
    from_z = [(block(t, x, zs[d]), w) for d in range(1, Z) for w in (at_x, at_t)]
    from_x = [(block(t, xo, zs[d]), at_t) for d in range(Z)]
    from_t = [block(to, xx, zs[d]) for xx in (x, xo) for d in range(Z)]
    routes_out = from_own + from_z + from_x

    def token_copy(n, k):
        b, where = routes_out[k]
        return pltpu.make_async_remote_copy(
            src_ref=xraw.at[n, b], dst_ref=xraw.at[n, b], send_sem=xs_sem.at[n, k], recv_sem=xr_sem.at[n, b],
            device_id=where, device_id_type=MESH)

    def arrived(n, b):
        pltpu.make_async_remote_copy(
            src_ref=xraw.at[n, b], dst_ref=xraw.at[n, b], send_sem=xs_sem.at[n, 0], recv_sem=xr_sem.at[n, b],
            device_id=at_t, device_id_type=MESH).wait_recv()

    def pass_z(n):
        k = len(from_own)
        for d in range(1, Z):
            arrived(n, block(t, x, zs[d]))
            token_copy(n, k).start()
            token_copy(n, k + 1).start()
            k += 2

    def pass_x(n):
        k = len(from_own) + len(from_z)
        for d in range(Z):
            arrived(n, block(t, xo, zs[d]))
            token_copy(n, k).start()
            k += 1

    for n in range(CN):
        for k in range(len(from_own)):
            token_copy(n, k).start()
    for c0, w in pieces(F, 512):
        acc_g[:, c0:c0 + w] = jnp.zeros((ROWS, w), jnp.float32)
        acc_u[:, c0:c0 + w] = jnp.zeros((ROWS, w), jnp.float32)
    pass_z(0)
    if CN > 1:
        pass_z(1)
    pass_x(0)

    @pl.loop(0, CN)
    def _(n):
        for b in from_t:
            arrived(n, b)

        @pl.loop(0, E * T // 2)
        def _(p):
            rows = pl.ds(pl.multiple_of(p * 2 * R, 2 * R), 2 * R)
            for j in range(STEPS):
                two = xraw[n, pl.ds(p * 2, 2), :, j * KB:(j + 1) * KB].astype(jnp.float32)
                xb[j, rows, :] = two.reshape(2 * R, KB).astype(jnp.bfloat16)

        for j in range(STEPS):
            k = n * STEPS + j
            slot = lax.rem(k, K_SLOTS)
            for cp, w_ref, acc in zip(gate_copies(k, slot), (wg, wu), (acc_g, acc_u)):
                cp.wait()
                for c0, w in pieces(F, 512):
                    acc[:, c0:c0 + w] += jnp.dot(
                        xb[j], w_ref[slot, :, c0:c0 + w], preferred_element_type=jnp.float32)

            @pl.when(k + K_SLOTS < KN)
            def _():
                for cp in gate_copies(k + K_SLOTS, slot):
                    cp.start()

            @pl.when(k + K_SLOTS == KN - 1)
            def _():
                for i in range(D_SLOTS):
                    down_copy(i, i).start()

            if j == 0:
                @pl.when(n + 1 < CN)
                def _():
                    pass_x(n + 1)

                @pl.when(n + 2 < CN)
                def _():
                    pass_z(n + 2)

    @pl.loop(0, E * T // 2)
    def _(p):
        rows = pl.ds(pl.multiple_of(p * 2 * R, 2 * R), 2 * R)
        two = xraw[0, pl.ds(p * 2, 2), :, CW:].astype(jnp.float32).reshape(2 * R, LANES)
        at = lax.broadcasted_iota(jnp.int32, (2 * R, LANES), 1)
        own = jnp.where((lax.rem(at, E) == e) & (at < 3 * E), two, 0.0)
        coef[rows, :] = jnp.broadcast_to(jnp.sum(own, axis=1, keepdims=True), (2 * R, LANES))

    for c0, w in pieces(F, 512):
        g = acc_g[:, c0:c0 + w]
        hid[:, c0:c0 + w] = (g / (1.0 + jnp.exp(-g)) * acc_u[:, c0:c0 + w]).astype(jnp.bfloat16)

    def copy_a(i):
        return pltpu.make_async_remote_copy(
            src_ref=part.at[i, to], dst_ref=got_a.at[i], send_sem=as_sem.at[i], recv_sem=ar_sem.at[i],
            device_id=at_t, device_id_type=MESH)

    def copy_b(i):
        return pltpu.make_async_remote_copy(
            src_ref=send_b.at[i], dst_ref=got_b.at[i], send_sem=bs_sem.at[i], recv_sem=br_sem.at[i],
            device_id=at_x, device_id_type=MESH)

    def copy_c(i, d):
        return pltpu.make_async_remote_copy(
            src_ref=send_c.at[i, zs[d]], dst_ref=got_c.at[i, d - 1],
            send_sem=cs_sem.at[i, d - 1], recv_sem=cr_sem.at[i, d - 1],
            device_id=at_z[d], device_id_type=MESH)

    LAG_A, LAG_B, LAG_C = 2, 5, 8

    @pl.loop(0, ND + LAG_C)
    def _(i):
        @pl.when(i < ND)
        def _():
            slot = lax.rem(i, D_SLOTS)
            down_copy(i, slot).wait()
            y = jnp.dot(hid[...], wd[slot], preferred_element_type=jnp.float32) * coef[:, 0:1]
            part[i] = y.reshape(T, E, R, NB).astype(jnp.bfloat16)
            copy_a(i).start()

            @pl.when(i + D_SLOTS < ND)
            def _():
                down_copy(i + D_SLOTS, slot).start()

        @pl.when((i >= LAG_A) & (i < ND + LAG_A))
        def _():
            j = i - LAG_A
            copy_a(j).wait_recv()
            theirs = pl.ds(xo * Z, Z)
            ours = pl.ds(x * Z, Z)
            send_b[j] = (part[j, t, theirs].astype(jnp.float32)
                         + got_a[j, theirs].astype(jnp.float32)).astype(jnp.bfloat16)
            copy_b(j).start()
            own_b[j] = part[j, t, ours].astype(jnp.float32) + got_a[j, ours].astype(jnp.float32)

        @pl.when((i >= LAG_B) & (i < ND + LAG_B))
        def _():
            j = i - LAG_B
            copy_b(j).wait_recv()
            send_c[j] = (own_b[j] + got_b[j].astype(jnp.float32)).astype(jnp.bfloat16)
            for d in range(1, Z):
                copy_c(j, d).start()

        @pl.when(i >= LAG_C)
        def _():
            j = i - LAG_C
            total = send_c[j, z].astype(jnp.float32)
            for d in range(1, Z):
                copy_c(j, d).wait_recv()
                total = total + got_c[j, d - 1].astype(jnp.float32)
            out_ref[:, pl.ds(pl.multiple_of(j * NB, NB), NB)] = total.astype(jnp.bfloat16)

    @pl.loop(0, CN)
    def _(n):
        for k in range(len(routes_out)):
            token_copy(n, k).wait_send()

    @pl.loop(0, ND)
    def _(i):
        copy_a(i).wait_send()
        copy_b(i).wait_send()
        for d in range(1, Z):
            copy_c(i, d).wait_send()


def fused_shards(tokens, routes, gate_fixed, w_gate, w_up, w_down):
    E, T = lax.axis_size("expert"), lax.axis_size("tensor")
    X = 2
    Z = E // X
    R, D = tokens.shape
    F = w_gate.shape[2]
    KB = divisor(D, 768, 256)
    NB = divisor(D, 768, 256)
    ND = D // NB
    CW = STEPS * KB
    CN = D // CW
    rows = E * T * R
    bf, f32 = jnp.bfloat16, jnp.float32
    vm = pltpu.VMEM
    dma = pltpu.SemaphoreType.DMA
    vmem, any_ = pl.BlockSpec(memory_space=vm), pl.BlockSpec(memory_space=pl.ANY)
    return pl.pallas_call(
        functools.partial(fused_kernel, Z, X, T, KB, NB),
        out_shape=jax.ShapeDtypeStruct((R, D), bf),
        in_specs=[vmem, vmem, vmem, any_, any_, any_],
        out_specs=vmem,
        scratch_shapes=[
            vm((CN, E * T, R, CW + LANES), bf),
            vm((STEPS, rows, KB), bf),
            vm((rows, LANES), f32),
            vm((K_SLOTS, KB, F), bf),
            vm((K_SLOTS, KB, F), bf),
            vm((D_SLOTS, F, NB), bf),
            vm((rows, F), f32),
            vm((rows, F), f32),
            vm((rows, F), bf),
            vm((ND, T, E, R, NB), bf),
            vm((ND, E, R, NB), bf),
            vm((ND, Z, R, NB), bf),
            vm((ND, Z, R, NB), f32),
            vm((ND, Z, R, NB), bf),
            vm((ND, Z, R, NB), bf),
            vm((ND, Z - 1, R, NB), bf),
            dma((K_SLOTS,)), dma((K_SLOTS,)), dma((D_SLOTS,)),
            dma((CN, E * T - 1)), dma((CN, E * T)),
            dma((ND,)), dma((ND,)), dma((ND,)), dma((ND,)), dma((ND, Z - 1)), dma((ND, Z - 1)),
        ],
        compiler_params=pltpu.CompilerParams(
            collective_id=0, has_side_effects=True, vmem_limit_bytes=61 * 1024 * 1024),
        cost_estimate=pl.CostEstimate(
            flops=6 * rows * D * F, bytes_accessed=6 * D * F, transcendentals=rows * F),
    )(tokens, routes, gate_fixed, w_gate, w_up, w_down)


def slot_table(route_block, n_experts):
    flat_ids = route_block.reshape(-1)
    onehot = (flat_ids[:, None] == jnp.arange(n_experts, dtype=jnp.int32)[None, :]).astype(
        jnp.int32
    )
    earlier = jnp.cumsum(onehot, axis=0) - onehot
    slot_pos = jnp.sum(earlier * onehot, axis=1)
    target = flat_ids * CAP + slot_pos
    owner_row = jnp.arange(flat_ids.shape[0], dtype=jnp.int32) // route_block.shape[1]
    source = jnp.full((n_experts * CAP,), -1, jnp.int32).at[target].set(owner_row)
    return (source, target)


def pick_rows(table, source):
    picked = jnp.take(table, jnp.maximum(source, 0), axis=0)
    return jnp.where((source >= 0)[..., None], picked, jnp.zeros_like(picked))


def shards(tokens, routes, gate_fixed, w_gate, w_up, w_down):
    n_experts = lax.axis_size("expert")
    model_width = tokens.shape[1]
    gate_mat = w_gate[0]
    up_mat = w_up[0]
    down_mat = w_down[0]
    source, target = slot_table(routes, n_experts)
    outgoing = pick_rows(tokens, source.reshape(n_experts, CAP))
    arrived = lax.all_to_all(outgoing, "expert", split_axis=0, concat_axis=0, tiled=True)
    row_piece = lax.all_gather(arrived.reshape(-1, model_width), "tensor", axis=0, tiled=True)
    gate_val = jnp.dot(row_piece, gate_mat, preferred_element_type=jnp.float32)
    up_val = jnp.dot(row_piece, up_mat, preferred_element_type=jnp.float32)
    hidden = (jax.nn.silu(gate_val) * up_val).astype(jnp.bfloat16)
    shared_sum = lax.psum_scatter(
        jnp.dot(hidden, down_mat, preferred_element_type=jnp.float32).astype(jnp.bfloat16),
        "tensor",
        scatter_dimension=0,
        tiled=True,
    )
    expert_rows = shared_sum.reshape(n_experts, CAP, model_width)
    returned = lax.all_to_all(expert_rows, "expert", split_axis=0, concat_axis=0, tiled=True)
    chosen = jnp.take(returned.reshape(-1, model_width), target, axis=0)
    chosen = chosen.reshape(tokens.shape[0], routes.shape[1], model_width)
    fixed_val = gate_fixed.astype(jnp.float32)
    mix_weights = fixed_val / jnp.sum(fixed_val, axis=1, keepdims=True)
    mixed = jnp.sum(chosen.astype(jnp.float32) * mix_weights[:, :, None], axis=1)
    return mixed.astype(jnp.bfloat16)


def solution(mesh):
    placed = (
        P(("group", "expert", "tensor"), None),
        P(("group", "expert", "tensor"), None),
        P(("group", "expert", "tensor"), None),
        P("expert", None, "tensor"),
        P("expert", None, "tensor"),
        P("expert", "tensor", None),
    )
    fits = (mesh.shape["tensor"] == 2 and mesh.shape["expert"] % 4 == 0)
    return jax.shard_map(
        fused_shards if fits else shards,
        mesh=mesh,
        in_specs=placed,
        out_specs=P(("group", "expert", "tensor"), None),
        check_vma=False,
    )
```
